32 devices in a mesh: groups: 2 (over y), space: 16 (over z, x, core).
Axes of the slice: x: 2, y: 2, z: 4, core: 2. Of those that a mesh axis runs over, the one named last changes fastest.
Arguments:
- features: bfloat16 [16384, 256], P(('groups', 'space')), parts along dimension 0, may hold values from -6 to 6
- positions: float32 [3, 16384], P(None, ('groups', 'space')), parts along dimension 1, may hold values from 0 to 1
- k_index: int32 [3, 2048], replicated, may hold values from -8 to 8
- k_filter: bfloat16 [2048, 256], replicated, may hold values from 0.0049743652 to 0.049804688
- w_in: bfloat16 [256, 256], replicated, may hold values from -0.375 to 0.375
- w_out: bfloat16 [256, 256], replicated, may hold values from -0.375 to 0.375
- w_msg: bfloat16 [256, 256], replicated, may hold values from -0.375 to 0.375
- w_short: bfloat16 [256, 256], replicated, may hold values from -0.375 to 0.375
- gamma: float32 [256], replicated, may hold values from 0.02 to 0.5
- ghost_index: int32 [64, 128], P(('groups', 'space')), parts along dimension 0, may hold values from 0 to 511, as said below
- atom_count: int32 [32], P(('groups', 'space')), parts along dimension 0, may hold values from 256 to 512, as said below
- edge_src: int32 [262144], P(('groups', 'space')), parts along dimension 0, may hold values from 0 to 767
- edge_dist: float32 [262144], P(('groups', 'space')), parts along dimension 0, may hold values from 0.5 to 5
- cotangent: bfloat16 [16384, 256], P(('groups', 'space')), parts along dimension 0, may hold values from -6 to 6
Outputs:
- mixed: bfloat16 [16384, 256], P(('groups', 'space')), parts along dimension 0
- feature_grad: bfloat16 [16384, 256], P(('groups', 'space')), parts along dimension 0
The draws below stay inside these ranges and needn't reach their ends.
There are 2 independent parts, one for each index of `groups`. The reference program is written for one: setup_inputs(seed, part) draws one part's arguments, and reference() takes and returns one part's arrays. A program takes and returns all parts, laid end to end along the dimension named above; an argument that names none is the same for every part. Nothing has to cross between parts.
Inputs may be any that keep to these rules, and one draw needn't show every extreme that they name: `ghost_index`: within each row the 128 slots are distinct. `atom_count`: some domain of every cell is full.
All inputs are finite; a program needn't handle non-finite values.
Results may differ from the reference program's by a relative error of at most 0.0065.
Values may be sent and summed in bfloat16 or wider, within the bound.
A program may use at most 128 MiB of HBM per device.

```python
import math
import jax
import jax.numpy as jnp
from jax import lax

C = 256
KV = 2048
AT_DEV = 512
NEIGH = 16
EBLOCKS = 4
GHOST = 128
TAB = 768
ATOMS = 8192
EDGES = 131072
N_SPACE = 16


def draw_ghost_index(key, part):
    key = jax.random.fold_in(key, 11)
    keys = jax.random.split(key, 2 * N_SPACE)
    picks = jax.vmap(lambda sub: jax.random.permutation(sub, AT_DEV)[:GHOST])(keys)
    return picks.astype(jnp.int32)


def draw_atom_count(key, part):
    key = jax.random.fold_in(key, 23)
    first, second = jax.random.split(key)
    counts = jax.random.randint(first, (N_SPACE,), AT_DEV // 2, AT_DEV + 1)
    fullest = jax.random.randint(second, (), 0, N_SPACE)
    counts = jnp.where(jnp.arange(N_SPACE) == fullest, AT_DEV, counts)
    return counts.astype(jnp.int32)


def touch_ends(result, rng, low, top_value):
    index_at = [jax.random.randint(jax.random.fold_in(rng, axis), (), 0, length) for axis, length in enumerate(result.shape)]
    longest = result.shape.index(max(result.shape))
    beside = index_at[:longest] + [(index_at[longest] + 1) % result.shape[longest]] + index_at[longest + 1:]
    return result.at[tuple(index_at)].set(low).at[tuple(beside)].set(top_value)


def shard_levels(key, shape, cuts, low, largest):
    factor_of, own = 1.0, jax.random.fold_in(key, 6)
    for dim, shards_of in cuts:
        steps = jnp.exp(jax.random.uniform(jax.random.fold_in(own, dim), (shards_of,), jnp.float32, low / len(cuts), largest / len(cuts)))
        factor_of = factor_of * jnp.repeat(steps, shape[dim] // shards_of).reshape([-1 if axis == dim else 1 for axis in range(len(shape))])
    return factor_of


def centred(key, extent, spread, most, cuts=(), kind=jnp.bfloat16):
    entries = spread * jax.random.normal(key, extent, jnp.float32)
    if cuts:
        entries = entries * shard_levels(key, extent, cuts, -0.22, 0.18)
    return jnp.clip(entries, -most, most).astype(kind)


def setup_inputs(seed: int = 0, part: int = 0) -> dict:
    key_of = jax.random.split(jax.random.key(seed), 15)
    part_splits = jax.random.split(jax.random.fold_in(key_of[14], part), 15)
    features = centred(part_splits[0], (ATOMS, C), 1.0, 6.0, ((0, 16),))
    positions = jnp.clip(1.0 * jax.random.uniform(part_splits[1], (3, ATOMS), jnp.float32) ** shard_levels(part_splits[1], (3, ATOMS), ((1, 16),), -0.2, 0.2), 0.0, 1.0)
    k_index = touch_ends(jax.random.randint(key_of[2], (3, KV), -8, 9), jax.random.fold_in(key_of[2], 1), -8, 8).astype(jnp.int32)
    k_filter = jnp.clip(jnp.exp(jax.random.uniform(key_of[3], (KV, C), jnp.float32, math.log(0.0049743652), math.log(0.049804688))), 0.0049743652, 0.049804688).astype(jnp.bfloat16)
    w_in = centred(key_of[4], (C, C), C ** -0.5, 0.375)
    w_out = centred(key_of[5], (C, C), C ** -0.5, 0.375)
    w_msg = centred(key_of[6], (C, C), C ** -0.5, 0.375)
    w_short = centred(key_of[7], (C, C), C ** -0.5, 0.375)
    gamma = jnp.clip(jnp.exp(jax.random.uniform(key_of[8], (C,), jnp.float32, math.log(0.02), math.log(0.5))), 0.02, 0.5)
    ghost_index = draw_ghost_index(jax.random.fold_in(jax.random.fold_in(key_of[14], part), 71), part)
    atom_count = draw_atom_count(jax.random.fold_in(jax.random.fold_in(key_of[14], part), 71), part)
    edge_src = touch_ends(jax.random.randint(part_splits[11], (EDGES,), 0, TAB), jax.random.fold_in(part_splits[11], 1), 0, TAB - 1).astype(jnp.int32)
    edge_dist = jnp.clip(0.5 + 4.5 * jax.random.uniform(part_splits[12], (EDGES,), jnp.float32) ** shard_levels(part_splits[12], (EDGES,), ((0, 16),), -0.2, 0.2), 0.5, 5.0)
    cotangent = centred(part_splits[13], (ATOMS, C), 1.0, 6.0, ((0, 16),))
    return dict(features=features, positions=positions, k_index=k_index, k_filter=k_filter, w_in=w_in, w_out=w_out, w_msg=w_msg, w_short=w_short, gamma=gamma, ghost_index=ghost_index, atom_count=atom_count, edge_src=edge_src, edge_dist=edge_dist, cotangent=cotangent)


def silu_grad(value):
    sig = jax.nn.sigmoid(value)
    return sig * (1.0 + value * (1.0 - sig))

def phases(coords, k_index):
    kfloat = k_index.astype(jnp.float32)
    angle = coords[0][:, None] * kfloat[0][None, :] + coords[1][:, None] * kfloat[1][None, :]
    angle = 2.0 * math.pi * (angle + coords[2][:, None] * kfloat[2][None, :])
    return (jnp.cos(angle).astype(jnp.bfloat16), jnp.sin(angle).astype(jnp.bfloat16))

def dot_lead(left, right):
    return lax.dot_general(left, right, (((0,), (0,)), ((), ())), preferred_element_type=jnp.float32)

def dot_trail(left, right):
    return lax.dot_general(left, right, (((1,), (1,)), ((), ())), preferred_element_type=jnp.float32)

def edge_filter(dist, alive, gamma):
    smooth = 0.5 * (jnp.cos(math.pi * dist / 5.0) + 1.0)
    return (alive * smooth)[:, None] * jnp.exp(-gamma[None, :] * (dist * dist)[:, None])

def short_range(table_rows, src, dist, alive_edges, gamma):
    width = table_rows.shape[1]

    def step(carry, pieces):
        source, length, alive = pieces
        radial = edge_filter(length, alive, gamma)
        message = table_rows[source].astype(jnp.float32) * radial
        return (carry, lax.optimization_barrier(jnp.sum(message.reshape(-1, NEIGH, width), axis=1)))
    blocks = (src.reshape(EBLOCKS, -1), dist.reshape(EBLOCKS, -1), alive_edges.reshape(EBLOCKS, -1))
    _, parts = lax.scan(step, jnp.zeros((), jnp.float32), blocks)
    return parts.reshape(-1, width)

def short_back(grad_agg, src, dist, alive_edges, gamma, n_rows):
    width = grad_agg.shape[1]

    def step(total, pieces):
        source, length, alive, grad_rows = pieces
        radial = edge_filter(length, alive, gamma)
        expanded = jnp.repeat(grad_rows, NEIGH, axis=0)
        term = (expanded * radial).astype(jnp.bfloat16)
        term = lax.optimization_barrier(term).astype(jnp.float32)
        return (total + jax.ops.segment_sum(term, source, num_segments=n_rows), None)
    blocks = (src.reshape(EBLOCKS, -1), dist.reshape(EBLOCKS, -1), alive_edges.reshape(EBLOCKS, -1), grad_agg.reshape(EBLOCKS, -1, width))
    total, _ = lax.scan(step, jnp.zeros((n_rows, width), jnp.float32), blocks)
    return total

def reference(features, positions, k_index, k_filter, w_in, w_out, w_msg, w_short, gamma, ghost_index, atom_count, edge_src, edge_dist, cotangent):
    width = features.shape[1]
    domains = N_SPACE
    feats = features.reshape(domains, AT_DEV, width)
    live = jnp.arange(AT_DEV)[None, :] < atom_count[:, None]
    masked = feats * live[:, :, None].astype(features.dtype)
    coords = positions.reshape(3, domains, AT_DEV).transpose(1, 0, 2)
    proj = jnp.dot(masked.reshape(-1, width), w_in, preferred_element_type=jnp.float32).astype(jnp.bfloat16)
    proj = proj.reshape(domains, AT_DEV, width)
    scale = 1.0 / math.sqrt(ATOMS)
    filt_both = jnp.concatenate([k_filter, k_filter], axis=1).astype(jnp.float32)

    def add_factor(total, pieces):
        place, rows = pieces
        cosines, sines = phases(place, k_index)
        return (total + jnp.concatenate([dot_lead(cosines, rows), dot_lead(sines, rows)], axis=1), None)
    factor, _ = lax.scan(add_factor, jnp.zeros((KV, 2 * width), jnp.float32), (coords, proj))
    filtered = (filt_both * factor * scale).astype(jnp.bfloat16)
    grad_live = cotangent.reshape(domains, AT_DEV, width) * live[:, :, None].astype(cotangent.dtype)

    def long_pass(total, pieces):
        place, upstream = pieces
        cosines, sines = phases(place, k_index)
        wave = jnp.dot(cosines, filtered[:, :width], preferred_element_type=jnp.float32)
        wave = wave + jnp.dot(sines, filtered[:, width:], preferred_element_type=jnp.float32)
        act = jax.nn.silu(wave).astype(jnp.bfloat16)
        long_out = jnp.dot(act, w_out, preferred_element_type=jnp.float32)
        grad_wave = (dot_trail(upstream, w_out) * silu_grad(wave)).astype(jnp.bfloat16)
        part = jnp.concatenate([dot_lead(cosines, grad_wave), dot_lead(sines, grad_wave)], axis=1)
        return (total + part, long_out)
    grad_factor, long_out = lax.scan(long_pass, jnp.zeros((KV, 2 * width), jnp.float32), (coords, grad_live))
    grad_filtered = (filt_both * grad_factor * scale).astype(jnp.bfloat16)

    def long_back(place):
        cosines, sines = phases(place, k_index)
        grad_proj = jnp.dot(cosines, grad_filtered[:, :width], preferred_element_type=jnp.float32)
        grad_proj = grad_proj + jnp.dot(sines, grad_filtered[:, width:], preferred_element_type=jnp.float32)
        return dot_trail(grad_proj.astype(jnp.bfloat16), w_in)
    grad_long = lax.map(long_back, coords)
    slots = ghost_index.reshape(domains, 2, GHOST)
    sent = jax.vmap(lambda rows, picks: rows[picks])(masked, slots)
    lower = jnp.roll(sent[:, 1], 1, axis=0)
    upper = jnp.roll(sent[:, 0], -1, axis=0)
    table = jnp.concatenate([masked, lower, upper], axis=1)
    table_rows = jnp.dot(table.reshape(-1, width), w_msg, preferred_element_type=jnp.float32).astype(jnp.bfloat16)
    table_rows = table_rows.reshape(domains, TAB, width)
    sources = edge_src.reshape(domains, -1)
    lengths = edge_dist.reshape(domains, -1)
    alive_edges = jnp.repeat(live.astype(jnp.float32), NEIGH, axis=1)

    def short_pass(pieces):
        rows, source, length, alive, upstream = pieces
        agg = short_range(rows, source, length, alive, gamma)
        short_act = jax.nn.silu(agg).astype(jnp.bfloat16)
        short_out = jnp.dot(short_act, w_short, preferred_element_type=jnp.float32)
        grad_agg = dot_trail(upstream, w_short) * silu_grad(agg)
        grad_hw = short_back(grad_agg, source, length, alive, gamma, TAB).astype(jnp.bfloat16)
        return (short_out, dot_trail(grad_hw, w_msg))
    short_out, grad_table = lax.map(short_pass, (table_rows, sources, lengths, alive_edges, grad_live))
    from_below = jnp.roll(grad_table[:, AT_DEV + GHOST:], 1, axis=0)
    from_above = jnp.roll(grad_table[:, AT_DEV:AT_DEV + GHOST], -1, axis=0)
    grad_own = jax.vmap(lambda rows, picks, below, above: rows.at[picks[0]].add(below).at[picks[1]].add(above))(grad_table[:, :AT_DEV], slots, from_below, from_above)
    live_f = live[:, :, None].astype(jnp.float32)
    mixed = (live_f * (masked.astype(jnp.float32) + short_out + long_out)).astype(jnp.bfloat16)
    feature_grad = (live_f * (grad_live.astype(jnp.float32) + grad_long + grad_own)).astype(jnp.bfloat16)
    return (mixed.reshape(ATOMS, width), feature_grad.reshape(ATOMS, width))
```

```python
import functools
import math

import jax
import jax.numpy as jnp
from jax import lax
from jax.experimental import pallas as pl
from jax.experimental.pallas import tpu as pltpu
from jax.sharding import PartitionSpec as P

NEIGH = 16
QUAD = 4
ROWS = 16
F32 = jnp.float32
BF16 = jnp.bfloat16

COS_FIT = (1.0, -19.73920440673828, 64.93911743164062, -85.45014190673828, 60.16762924194336, -25.967599868774414, 6.528658390045166)
SIN_FIT = (6.283185005187988, -41.341590881347656, 81.59994506835938, -76.61447143554688, 41.3428840637207, -12.471243858337402)


def horner(square, coefs):
    result = jnp.full_like(square, coefs[-1])
    for coef in coefs[-2::-1]:
        result = result * square + coef
    return result


def dot(left, right):
    return jnp.dot(left, right, preferred_element_type=F32)


def dot_trail(left, right):
    return lax.dot_general(left, right, (((1,), (1,)), ((), ())), preferred_element_type=F32)


def sigmoid(value):
    return 1.0 / (1.0 + jnp.exp(-value))


def silu_grad(value):
    sig = sigmoid(value)
    return sig * (1.0 + value * (1.0 - sig))


def one_hot(ids, axis, extent):
    shape = (ids.shape[0], extent) if axis == 1 else (extent, ids.shape[1])
    return jnp.where(lax.broadcasted_iota(jnp.int32, shape, axis) == ids, 1.0, 0.0).astype(BF16)


def kernel(
    n,
    scale,
    feat_ref,
    pos_ref,
    kidx_ref,
    kfilt_ref,
    win_ref,
    wout_ref,
    wmsg_ref,
    wshort_ref,
    gamma_ref,
    ghost_ref,
    ghost_col_ref,
    count_ref,
    src_ref,
    src_row_ref,
    dist_ref,
    cot_ref,
    mixed_ref,
    grad_ref,
    phase,
    kcol,
    pos_all,
    quad_all,
    z_send,
    z_recv,
    z_all,
    z_own,
    sib_send,
    sib_recv,
    x_send,
    x_recv,
    table,
    hw,
    agg,
    grad_agg,
    grad_hw,
    ghost_send,
    ghost_back,
    masked_ref,
    glive_ref,
    wave_ref,
    long_ref,
    pos_sems,
    gather_sems,
    zr_sems,
    za_sems,
    quad_sems,
    ghost_sems,
):
    zs = n // QUAD
    at, width = feat_ref.shape
    kq = kidx_ref.shape[1] // QUAD
    kc = kq // zs
    ghost = ghost_ref.shape[1]
    me = lax.axis_index("space")
    q = lax.rem(me, QUAD)
    z = lax.div(me, QUAD)
    base = z * QUAD
    sib = q + 1 - 2 * lax.rem(q, 2)
    xp = lax.rem(q + 2, QUAD)
    diag = lax.rem(sib + 2, QUAD)
    right = lax.rem(me + 1, n)
    left = lax.rem(me + n - 1, n)

    def z_peer(step):
        return lax.rem(z + step, zs)

    barrier = pltpu.get_barrier_semaphore()
    peers = [base + sib, base + xp, left, right] + [z_peer(r) * QUAD + q for r in range(1, zs)]
    for peer in peers:
        pl.semaphore_signal(
            barrier, inc=1, device_id={"space": peer}, device_id_type=pl.DeviceIdType.MESH
        )

    def push(src, dst, sems, index, peer):
        return pltpu.make_async_remote_copy(
            src_ref=src,
            dst_ref=dst,
            send_sem=sems.at[(0,) + index],
            recv_sem=sems.at[(1,) + index],
            device_id={"space": peer},
            device_id_type=pl.DeviceIdType.MESH,
        )

    live = lax.broadcasted_iota(jnp.int32, (at, width), 0) < count_ref[0]
    live_f = jnp.where(live, 1.0, 0.0)
    masked = (feat_ref[...].astype(F32) * live_f).astype(BF16)
    masked_ref[...] = masked
    glive_ref[...] = (cot_ref[...].astype(F32) * live_f).astype(BF16)
    table[pl.ds(0, at), :] = masked
    quad_all[0, q] = dot(masked, win_ref[...]).astype(BF16)
    pos_all[q] = jnp.concatenate([pos_ref[...], jnp.zeros((5, at), F32)], axis=0)
    ghost_send[0, 0] = dot(one_hot(ghost_col_ref[:, 0:1], 1, at), masked).astype(BF16)
    ghost_send[0, 1] = dot(one_hot(ghost_col_ref[:, 1:2], 1, at), masked).astype(BF16)

    pl.semaphore_wait(barrier, len(peers))

    pos_copies = [
        push(pos_all.at[q], pos_all.at[q], pos_sems, (0,), base + sib),
        push(pos_all.at[q], pos_all.at[q], pos_sems, (1,), base + xp),
        push(pos_all.at[xp], pos_all.at[xp], pos_sems, (2,), base + sib),
    ]

    def gather_copies(rnd):
        buf = quad_all.at[rnd]
        return [
            push(buf.at[q], buf.at[q], gather_sems, (rnd, 0), base + sib),
            push(buf.at[q], buf.at[q], gather_sems, (rnd, 1), base + xp),
            push(buf.at[xp], buf.at[xp], gather_sems, (rnd, 2), base + sib),
        ]

    proj_copies = gather_copies(0)
    ghosts_out = [
        push(ghost_send.at[0, 0], table.at[pl.ds(at + ghost, ghost)], ghost_sems, (0, 0), left),
        push(ghost_send.at[0, 1], table.at[pl.ds(at, ghost)], ghost_sems, (0, 1), right),
    ]
    pos_copies[0].start()
    pos_copies[1].start()
    proj_copies[1].start()
    proj_copies[0].start()
    ghosts_out[0].start()
    ghosts_out[1].start()

    kq_rows = kidx_ref[:, pl.ds(pl.multiple_of(q * kq, 128), kq)].astype(F32)
    kcol[...] = jnp.concatenate([kq_rows, jnp.zeros((5, kq), F32)], axis=0).T

    def fill_phase(slot):
        columns = pl.ds(pl.multiple_of(slot * at, 128), at)
        p0 = pos_all[slot, 0:1, :]
        p1 = pos_all[slot, 1:2, :]
        p2 = pos_all[slot, 2:3, :]

        def body(i, carry):
            first = pl.multiple_of(i * ROWS, ROWS)
            ks = kcol[pl.ds(first, ROWS), :]
            turn = ks[:, 0:1] * p0 + ks[:, 1:2] * p1 + ks[:, 2:3] * p2
            turn = turn - jnp.round(turn)
            square = turn * turn
            row = pl.multiple_of(first + lax.div(first, kc) * kc, ROWS)
            phase[pl.ds(row, ROWS), columns] = horner(square, COS_FIT).astype(BF16)
            row = pl.multiple_of(row + kc, ROWS)
            phase[pl.ds(row, ROWS), columns] = (turn * horner(square, SIN_FIT)).astype(BF16)
            return carry

        lax.fori_loop(0, kq // ROWS, body, 0)

    fill_phase(q)
    pos_copies[0].wait()
    pos_copies[1].wait()
    pos_copies[2].start()
    fill_phase(sib)
    fill_phase(xp)
    pos_copies[2].wait()
    proj_copies[1].wait()
    proj_copies[2].start()
    fill_phase(diag)

    def z_start(rnd):
        rows = quad_all[rnd].reshape(QUAD * at, width)
        copies = []
        for r in list(range(1, zs)) + [0]:
            j = z_peer(r)
            part = dot(phase[pl.ds(pl.multiple_of(j * 2 * kc, ROWS), 2 * kc), :], rows)
            if r == 0:
                z_own[...] = part
            else:
                z_send[rnd, j] = part.astype(BF16)
                copy = push(z_send.at[rnd, j], z_recv.at[rnd, z], zr_sems, (rnd, r - 1), j * QUAD + q)
                copy.start()
                copies.append(copy)
        return copies

    def z_middle(rnd, copies):
        total = z_own[...]
        for r in range(1, zs):
            copies[r - 1].wait()
            total = total + z_recv[rnd, lax.rem(z + zs - r, zs)].astype(F32)
        filt = kfilt_ref[pl.ds(pl.multiple_of(q * kq + z * kc, ROWS), kc), :].astype(F32)
        z_all[rnd, z] = (jnp.concatenate([filt, filt], axis=0) * total * scale).astype(BF16)
        out = []
        for r in range(1, zs):
            copy = push(z_all.at[rnd, z], z_all.at[rnd, z], za_sems, (rnd, r - 1), z_peer(r) * QUAD + q)
            copy.start()
            out.append(copy)
        return out

    def z_end(rnd, copies):
        for copy in copies:
            copy.wait()
        spectrum = z_all[rnd].reshape(2 * kq, width).T

        def section(slot):
            return dot(spectrum, phase[:, pl.ds(pl.multiple_of(slot * at, 128), at)])

        across = push(sib_send.at[rnd, 1], sib_recv.at[rnd, 1], quad_sems, (rnd, 0), base + sib)
        beside = push(sib_send.at[rnd, 0], sib_recv.at[rnd, 0], quad_sems, (rnd, 1), base + sib)
        over = push(x_send.at[rnd], x_recv.at[rnd], quad_sems, (rnd, 2), base + xp)
        sib_send[rnd, 1] = section(diag).astype(BF16)
        across.start()
        part = section(xp)
        across.wait()
        x_send[rnd] = (part + sib_recv[rnd, 1].astype(F32)).astype(BF16)
        over.start()
        sib_send[rnd, 0] = section(sib).astype(BF16)
        beside.start()
        part = section(q)
        beside.wait()
        part = part + sib_recv[rnd, 0].astype(F32)
        over.wait()
        return (part + x_recv[rnd].astype(F32)).T

    proj_copies[0].wait()
    proj_copies[2].wait()
    reduce_copies = z_start(0)

    dist = dist_ref[...]
    dist_sq = dist * dist
    turn = dist * 0.1
    live_col = jnp.where(
        lax.broadcasted_iota(jnp.int32, (at, NEIGH), 0) < count_ref[0], 1.0, 0.0
    )
    smooth = live_col * (0.5 * (horner(turn * turn, COS_FIT) + 1.0))
    gamma_neg = -gamma_ref[...]

    def radial(j):
        return smooth[:, j : j + 1] * jnp.exp(gamma_neg * dist_sq[:, j : j + 1])

    ghosts_out[0].wait()
    ghosts_out[1].wait()
    hw[...] = dot(table[...], wmsg_ref[...]).astype(BF16)
    for j in range(NEIGH):
        message = dot(one_hot(src_ref[:, j : j + 1], 1, at + 2 * ghost), hw[...]) * radial(j)
        agg[...] = message if j == 0 else agg[...] + message

    spread_copies = z_middle(0, reduce_copies)

    agg_now = agg[...]
    grad_agg[...] = dot_trail(glive_ref[...], wshort_ref[...]) * silu_grad(agg_now)
    for j in range(NEIGH):
        term = (grad_agg[...] * radial(j)).astype(BF16)
        part = dot(one_hot(src_row_ref[j : j + 1, :], 0, at + 2 * ghost), term)
        grad_hw[...] = part if j == 0 else grad_hw[...] + part

    wave = z_end(0, spread_copies)
    grad_wave = dot_trail(glive_ref[...], wout_ref[...]) * silu_grad(wave)
    quad_all[1, q] = grad_wave.astype(BF16)
    back_copies = gather_copies(1)
    back_copies[1].start()
    back_copies[0].start()

    grad_table = dot_trail(grad_hw[...].astype(BF16), wmsg_ref[...])
    ghost_send[1, 0] = grad_table[at : at + ghost].astype(BF16)
    ghost_send[1, 1] = grad_table[at + ghost :].astype(BF16)
    ghosts_back = [
        push(ghost_send.at[1, 0], ghost_back.at[1], ghost_sems, (1, 0), left),
        push(ghost_send.at[1, 1], ghost_back.at[0], ghost_sems, (1, 1), right),
    ]
    back_copies[1].wait()
    back_copies[2].start()
    ghosts_back[0].start()
    ghosts_back[1].start()
    long_ref[...] = grad_table[:at]
    act = (wave * sigmoid(wave)).astype(BF16)
    short_act = (agg_now * sigmoid(agg_now)).astype(BF16)
    mixed = masked_ref[...].astype(F32) + dot(short_act, wshort_ref[...])
    mixed = mixed + dot(act, wout_ref[...])
    mixed_ref[...] = (live_f * mixed).astype(BF16)
    back_copies[0].wait()
    back_copies[2].wait()
    reduce_copies = z_start(1)

    ghosts_back[0].wait()
    ghosts_back[1].wait()
    own = long_ref[...]
    own = own + dot(one_hot(ghost_ref[0:1, :], 0, at), ghost_back[0])
    own = own + dot(one_hot(ghost_ref[1:2, :], 0, at), ghost_back[1])
    long_ref[...] = own + glive_ref[...].astype(F32)

    spread_copies = z_middle(1, reduce_copies)
    grad_proj = z_end(1, spread_copies).astype(BF16)
    total = long_ref[...] + dot_trail(grad_proj, win_ref[...])
    grad_ref[...] = (live_f * total).astype(BF16)


def shards(n, features, positions, k_index, k_filter, w_in, w_out, w_msg, w_short, gamma,
           ghost_index, atom_count, edge_src, edge_dist, cotangent):
    at, width = features.shape
    ghost = ghost_index.shape[1]
    kv = k_index.shape[1]
    zs = n // QUAD
    kq = kv // QUAD
    kc = kq // zs
    tab = at + 2 * ghost
    src = edge_src.reshape(at, NEIGH)
    vmem = pl.BlockSpec(memory_space=pltpu.VMEM)
    smem = pl.BlockSpec(memory_space=pltpu.SMEM)
    dma = pltpu.SemaphoreType.DMA
    return pl.pallas_call(
        functools.partial(kernel, n, 1.0 / math.sqrt(at * n)),
        out_shape=(
            jax.ShapeDtypeStruct((at, width), BF16),
            jax.ShapeDtypeStruct((at, width), BF16),
        ),
        in_specs=[vmem] * 11 + [smem] + [vmem] * 4,
        out_specs=(vmem, vmem),
        scratch_shapes=[
            pltpu.VMEM((2 * kq, QUAD * at), BF16),
            pltpu.VMEM((kq, 8), F32),
            pltpu.VMEM((QUAD, 8, at), F32),
            pltpu.VMEM((2, QUAD, at, width), BF16),
            pltpu.VMEM((2, zs, 2 * kc, width), BF16),
            pltpu.VMEM((2, zs, 2 * kc, width), BF16),
            pltpu.VMEM((2, zs, 2 * kc, width), BF16),
            pltpu.VMEM((2 * kc, width), F32),
            pltpu.VMEM((2, 2, width, at), BF16),
            pltpu.VMEM((2, 2, width, at), BF16),
            pltpu.VMEM((2, width, at), BF16),
            pltpu.VMEM((2, width, at), BF16),
            pltpu.VMEM((tab, width), BF16),
            pltpu.VMEM((tab, width), BF16),
            pltpu.VMEM((at, width), F32),
            pltpu.VMEM((at, width), F32),
            pltpu.VMEM((tab, width), F32),
            pltpu.VMEM((2, 2, ghost, width), BF16),
            pltpu.VMEM((2, ghost, width), BF16),
            pltpu.VMEM((at, width), BF16),
            pltpu.VMEM((at, width), BF16),
            pltpu.VMEM((at, width), F32),
            pltpu.VMEM((at, width), F32),
            dma((2, 3)),
            dma((2, 2, 3)),
            dma((2, 2, zs - 1)),
            dma((2, 2, zs - 1)),
            dma((2, 2, 3)),
            dma((2, 2, 2)),
        ],
        compiler_params=pltpu.CompilerParams(
            collective_id=0, has_side_effects=True, vmem_limit_bytes=52 * 1024 * 1024
        ),
    )(
        features,
        positions,
        k_index,
        k_filter,
        w_in,
        w_out,
        w_msg,
        w_short,
        gamma.reshape(1, width),
        ghost_index,
        ghost_index.T,
        atom_count,
        src,
        src.T,
        edge_dist.reshape(at, NEIGH),
        cotangent,
    )


def solution(mesh):
    both = ("groups", "space")
    in_specs = (P(both, None), P(None, both)) + (P(),) * 7
    in_specs = in_specs + (P(both, None), P(both), P(both), P(both), P(both, None))
    out_specs = (P(both, None), P(both, None))
    return jax.shard_map(
        functools.partial(shards, mesh.shape["space"]),
        mesh=mesh,
        in_specs=in_specs,
        out_specs=out_specs,
        check_vma=False,
    )
```

```python
import functools
import math

import jax
import jax.numpy as jnp
from jax import lax
from jax.experimental import pallas as pl
from jax.experimental.pallas import tpu as pltpu
from jax.sharding import PartitionSpec as P

NEIGH = 16
QUAD = 4
HALVES = 2
ROWS = 16
WHOLE = 1.5 * 2.0**23
F32 = jnp.float32
BF16 = jnp.bfloat16

COS_FIT = (0.9999992251396179, -19.738981246948242, 64.92865753173828, -85.27162170410156, 58.79049301147461, -21.07110595703125)
SIN_FIT = (6.283185005187988, -41.341590881347656, 81.59994506835938, -76.61447143554688, 41.3428840637207, -12.471243858337402)


def horner(square, coefs):
    result = jnp.full_like(square, coefs[-1])
    for coef in coefs[-2::-1]:
        result = result * square + coef
    return result


def dot(left, right):
    return jnp.dot(left, right, preferred_element_type=F32)


def dot_trail(left, right):
    return lax.dot_general(left, right, (((1,), (1,)), ((), ())), preferred_element_type=F32)


def sigmoid(value):
    return 1.0 / (1.0 + jnp.exp(-value))


def silu_grad(value):
    sig = sigmoid(value)
    return sig * (1.0 + value * (1.0 - sig))


def one_hot(ids, axis, extent):
    shape = (ids.shape[0], extent) if axis == 1 else (extent, ids.shape[1])
    return jnp.where(lax.broadcasted_iota(jnp.int32, shape, axis) == ids, 1.0, 0.0).astype(BF16)


def kernel(
    n,
    scale,
    feat_ref,
    pos_ref,
    kidx_ref,
    kfilt_ref,
    win_ref,
    wout_ref,
    wmsg_ref,
    wshort_ref,
    gamma_ref,
    ghost_ref,
    ghost_col_ref,
    count_ref,
    src_ref,
    src_row_ref,
    dist_ref,
    cot_ref,
    mixed_ref,
    grad_ref,
    phase,
    kcol,
    pos_all,
    quad_all,
    z_send,
    z_recv,
    z_all,
    z_own,
    sib_send,
    sib_recv,
    x_send,
    x_recv,
    table,
    hw,
    agg,
    grad_agg,
    grad_hw,
    ghost_send,
    ghost_back,
    masked_ref,
    glive_ref,
    wave_ref,
    long_ref,
    upstream_ref,
    mine,
    pos_sems,
    gather_sems,
    zr_sems,
    za_sems,
    quad_sems,
    ghost_sems,
):
    zs = n // QUAD
    at, width = feat_ref.shape
    kq = kidx_ref.shape[1] // QUAD
    kc = kq // zs
    ghost = ghost_ref.shape[1]
    half = width // HALVES
    me = lax.axis_index("space")
    q = lax.rem(me, QUAD)
    z = lax.div(me, QUAD)
    base = z * QUAD
    sib = q + 1 - 2 * lax.rem(q, 2)
    xp = lax.rem(q + 2, QUAD)
    diag = lax.rem(sib + 2, QUAD)
    right = lax.rem(me + 1, n)
    left = lax.rem(me + n - 1, n)

    def z_peer(step):
        return lax.rem(z + step, zs)

    barrier = pltpu.get_barrier_semaphore()
    peers = [base + sib, base + xp, left, right] + [z_peer(r) * QUAD + q for r in range(1, zs)]
    for peer in peers:
        pl.semaphore_signal(
            barrier, inc=1, device_id={"space": peer}, device_id_type=pl.DeviceIdType.MESH
        )

    def push(src, dst, sems, index, peer):
        return pltpu.make_async_remote_copy(
            src_ref=src,
            dst_ref=dst,
            send_sem=sems.at[(0,) + index],
            recv_sem=sems.at[(1,) + index],
            device_id={"space": peer},
            device_id_type=pl.DeviceIdType.MESH,
        )

    live = lax.broadcasted_iota(jnp.int32, (at, width), 0) < count_ref[0]
    live_f = jnp.where(live, 1.0, 0.0)
    masked = (feat_ref[...].astype(F32) * live_f).astype(BF16)
    masked_ref[...] = masked
    pos_all[q] = jnp.concatenate([pos_ref[...], jnp.zeros((5, at), F32)], axis=0)
    proj = dot(masked, win_ref[...]).astype(BF16)
    for h in range(HALVES):
        quad_all[0, h, q] = proj[:, h * half : (h + 1) * half]

    pl.semaphore_wait(barrier, len(peers))

    pos_copies = [
        push(pos_all.at[q], pos_all.at[q], pos_sems, (0,), base + sib),
        push(pos_all.at[q], pos_all.at[q], pos_sems, (1,), base + xp),
        push(pos_all.at[xp], pos_all.at[xp], pos_sems, (2,), base + sib),
    ]

    def gather_copies(rnd, h):
        buf = quad_all.at[rnd, h]
        return [
            push(buf.at[q], buf.at[q], gather_sems, (rnd, h, 0), base + sib),
            push(buf.at[q], buf.at[q], gather_sems, (rnd, h, 1), base + xp),
            push(buf.at[xp], buf.at[xp], gather_sems, (rnd, h, 2), base + sib),
        ]

    pos_copies[1].start()
    pos_copies[0].start()
    gathers = [gather_copies(0, h) for h in range(HALVES)]
    for copies in gathers:
        copies[1].start()
        copies[0].start()

    table[pl.ds(0, at), :] = masked
    ghost_send[0, 0] = dot(one_hot(ghost_col_ref[:, 0:1], 1, at), masked).astype(BF16)
    ghost_send[0, 1] = dot(one_hot(ghost_col_ref[:, 1:2], 1, at), masked).astype(BF16)
    ghosts_out = [
        push(ghost_send.at[0, 0], table.at[pl.ds(at + ghost, ghost)], ghost_sems, (0, 0), left),
        push(ghost_send.at[0, 1], table.at[pl.ds(at, ghost)], ghost_sems, (0, 1), right),
    ]
    ghosts_out[0].start()
    ghosts_out[1].start()
    kq_rows = kidx_ref[:, pl.ds(pl.multiple_of(q * kq, 128), kq)].astype(F32)
    kcol[...] = jnp.concatenate([kq_rows, jnp.zeros((5, kq), F32)], axis=0).T
    glive_ref[...] = (cot_ref[...].astype(F32) * live_f).astype(BF16)
    pos_copies[1].wait()
    pos_copies[2].start()
    pos_copies[0].wait()
    upstream_ref[...] = dot_trail(glive_ref[...], wout_ref[...])
    grad_agg[...] = dot_trail(glive_ref[...], wshort_ref[...])
    pos_copies[2].wait()

    def fill_phase(j):
        def body(i, carry):
            first = pl.multiple_of(j * kc + i * ROWS, ROWS)
            ks = kcol[pl.ds(first, ROWS), :]
            row = pl.multiple_of(j * 2 * kc + i * ROWS, ROWS)
            k0 = jnp.broadcast_to(ks[:, 0:1], (ROWS, at))
            k1 = jnp.broadcast_to(ks[:, 1:2], (ROWS, at))
            k2 = jnp.broadcast_to(ks[:, 2:3], (ROWS, at))
            for slot in range(QUAD):
                columns = pl.ds(slot * at, at)
                turn = k0 * pos_all[slot, 0:1, :] + k1 * pos_all[slot, 1:2, :]
                turn = turn + k2 * pos_all[slot, 2:3, :]
                turn = turn - ((turn + WHOLE) - WHOLE)
                square = turn * turn
                phase[pl.ds(row, ROWS), columns] = horner(square, COS_FIT).astype(BF16)
                sines = (turn * horner(square, SIN_FIT)).astype(BF16)
                phase[pl.ds(pl.multiple_of(row + kc, ROWS), ROWS), columns] = sines
            return carry

        lax.fori_loop(0, kc // ROWS, body, 0)

    def z_part(rnd, h, r):
        j = z_peer(r)
        rows = quad_all[rnd, h].reshape(QUAD * at, half)
        part = dot(phase[pl.ds(pl.multiple_of(j * 2 * kc, ROWS), 2 * kc), :], rows)
        if r == 0:
            z_own[h] = part
            return []
        z_send[rnd, h, j] = part.astype(BF16)
        copy = push(
            z_send.at[rnd, h, j], z_recv.at[rnd, h, z], zr_sems, (rnd, h, r - 1), j * QUAD + q
        )
        copy.start()
        return [copy]

    def z_middle(rnd, h, copies):
        total = z_own[h]
        for r in range(1, zs):
            copies[r - 1].wait()
            total = total + z_recv[rnd, h, lax.rem(z + zs - r, zs)].astype(F32)
        first = pl.multiple_of(q * kq + z * kc, ROWS)
        filt = kfilt_ref[pl.ds(first, kc), h * half : (h + 1) * half].astype(F32)
        z_all[rnd, h, z] = (jnp.concatenate([filt, filt], axis=0) * total * scale).astype(BF16)
        out = []
        for r in range(1, zs):
            copy = push(
                z_all.at[rnd, h, z], z_all.at[rnd, h, z], za_sems, (rnd, h, r - 1), z_peer(r) * QUAD + q
            )
            copy.start()
            out.append(copy)
        return out

    def z_end(rnd, h, copies):
        for copy in copies:
            copy.wait()
        spectrum = z_all[rnd, h].reshape(2 * kq, half).T

        def section(slot):
            return dot(spectrum, phase[:, pl.ds(pl.multiple_of(slot * at, 128), at)])

        def sib_copy(k):
            return push(
                sib_send.at[rnd, h, k], sib_recv.at[rnd, h, k], quad_sems, (rnd, h, k), base + sib
            )

        across, beside = sib_copy(1), sib_copy(0)
        over = push(x_send.at[rnd, h], x_recv.at[rnd, h], quad_sems, (rnd, h, 2), base + xp)
        sib_send[rnd, h, 1] = section(diag).astype(BF16)
        across.start()
        part = section(xp)
        sib_send[rnd, h, 0] = section(sib).astype(BF16)
        beside.start()
        across.wait()
        x_send[rnd, h] = (part + sib_recv[rnd, h, 1].astype(F32)).astype(BF16)
        over.start()
        mine[h] = section(q)
        return beside, over

    def quad_sum(rnd, h, copies):
        copies[0].wait()
        copies[1].wait()
        total = mine[h] + sib_recv[rnd, h, 0].astype(F32)
        return (total + x_recv[rnd, h].astype(F32)).T

    def columns_of(h):
        return pl.ds(h * half, half)

    def back_start(h):
        wave = quad_sum(0, h, sums[h])
        wave_ref[:, columns_of(h)] = wave
        grad_wave = upstream_ref[:, columns_of(h)] * silu_grad(wave)
        quad_all[1, h, q] = grad_wave.astype(BF16)
        copies = gather_copies(1, h)
        copies[1].start()
        copies[0].start()
        return copies

    def forward_on(copies):
        copies[1].wait()
        copies[2].start()

    order = list(range(1, zs)) + [0]
    reduces = [[], []]
    for step, r in enumerate(order):
        fill_phase(z_peer(r))
        if step == 0:
            for copies in gathers:
                forward_on(copies)
            for copies in gathers:
                copies[0].wait()
                copies[2].wait()
        for h in range(HALVES):
            reduces[h] += z_part(0, h, r)

    spreads = [z_middle(0, h, reduces[h]) for h in range(HALVES)]

    dist = dist_ref[...]
    dist_sq = dist * dist
    turn = dist * 0.1
    live_col = jnp.where(
        lax.broadcasted_iota(jnp.int32, (at, NEIGH), 0) < count_ref[0], 1.0, 0.0
    )
    smooth = live_col * (0.5 * (horner(turn * turn, COS_FIT) + 1.0))
    gamma_neg = -gamma_ref[...]

    def radial(j):
        return smooth[:, j : j + 1] * jnp.exp(gamma_neg * dist_sq[:, j : j + 1])

    ghosts_out[0].wait()
    ghosts_out[1].wait()
    hw[...] = dot(table[...], wmsg_ref[...]).astype(BF16)
    for j in range(NEIGH):
        message = dot(one_hot(src_ref[:, j : j + 1], 1, at + 2 * ghost), hw[...]) * radial(j)
        agg[...] = message if j == 0 else agg[...] + message

    def short_back(first, last):
        for j in range(first, last):
            term = (grad_agg[...] * radial(j)).astype(BF16)
            part = dot(one_hot(src_row_ref[j : j + 1, :], 0, at + 2 * ghost), term)
            grad_hw[...] = part if j == 0 else grad_hw[...] + part

    sums = [z_end(0, 0, spreads[0])]
    grad_agg[...] = grad_agg[...] * silu_grad(agg[...])
    short_back(0, 4)
    sums.append(z_end(0, 1, spreads[1]))
    gathers = [back_start(0)]
    short_back(4, 6)
    gathers.append(back_start(1))
    reduces = []
    forward_on(gathers[0])
    gathers[0][0].wait()
    gathers[0][2].wait()
    reduces.append(sum([z_part(1, 0, r) for r in order], []))
    forward_on(gathers[1])
    gathers[1][0].wait()
    gathers[1][2].wait()
    reduces.append(sum([z_part(1, 1, r) for r in order], []))

    short_back(6, NEIGH)
    grad_table = dot_trail(grad_hw[...].astype(BF16), wmsg_ref[...])
    ghost_send[1, 0] = grad_table[at : at + ghost].astype(BF16)
    ghost_send[1, 1] = grad_table[at + ghost :].astype(BF16)
    ghosts_back = [
        push(ghost_send.at[1, 0], ghost_back.at[1], ghost_sems, (1, 0), left),
        push(ghost_send.at[1, 1], ghost_back.at[0], ghost_sems, (1, 1), right),
    ]
    ghosts_back[0].start()
    ghosts_back[1].start()
    long_ref[...] = grad_table[:at]
    spreads = [z_middle(1, h, reduces[h]) for h in range(HALVES)]

    wave = wave_ref[...]
    act = (wave * sigmoid(wave)).astype(BF16)
    short_act = (agg[...] * sigmoid(agg[...])).astype(BF16)
    mixed = masked_ref[...].astype(F32) + dot(short_act, wshort_ref[...])
    mixed = mixed + dot(act, wout_ref[...])
    mixed_ref[...] = (live_f * mixed).astype(BF16)
    ghosts_back[0].wait()
    ghosts_back[1].wait()
    own = long_ref[...]
    own = own + dot(one_hot(ghost_ref[0:1, :], 0, at), ghost_back[0])
    own = own + dot(one_hot(ghost_ref[1:2, :], 0, at), ghost_back[1])
    long_ref[...] = own + glive_ref[...].astype(F32)

    sums = [z_end(1, h, spreads[h]) for h in range(HALVES)]
    grad_proj = [quad_sum(1, h, sums[h]).astype(BF16) for h in range(HALVES)]
    total = long_ref[...] + dot_trail(jnp.concatenate(grad_proj, axis=1), win_ref[...])
    grad_ref[...] = (live_f * total).astype(BF16)


def shards(n, features, positions, k_index, k_filter, w_in, w_out, w_msg, w_short, gamma,
           ghost_index, atom_count, edge_src, edge_dist, cotangent):
    at, width = features.shape
    ghost = ghost_index.shape[1]
    kv = k_index.shape[1]
    zs = n // QUAD
    kq = kv // QUAD
    kc = kq // zs
    tab = at + 2 * ghost
    half = width // HALVES
    src = edge_src.reshape(at, NEIGH)
    vmem = pl.BlockSpec(memory_space=pltpu.VMEM)
    smem = pl.BlockSpec(memory_space=pltpu.SMEM)
    dma = pltpu.SemaphoreType.DMA
    return pl.pallas_call(
        functools.partial(kernel, n, 1.0 / math.sqrt(at * n)),
        out_shape=(
            jax.ShapeDtypeStruct((at, width), BF16),
            jax.ShapeDtypeStruct((at, width), BF16),
        ),
        in_specs=[vmem] * 11 + [smem] + [vmem] * 4,
        out_specs=(vmem, vmem),
        scratch_shapes=[
            pltpu.VMEM((2 * kq, QUAD * at), BF16),
            pltpu.VMEM((kq, 8), F32),
            pltpu.VMEM((QUAD, 8, at), F32),
            pltpu.VMEM((2, HALVES, QUAD, at, half), BF16),
            pltpu.VMEM((2, HALVES, zs, 2 * kc, half), BF16),
            pltpu.VMEM((2, HALVES, zs, 2 * kc, half), BF16),
            pltpu.VMEM((2, HALVES, zs, 2 * kc, half), BF16),
            pltpu.VMEM((HALVES, 2 * kc, half), F32),
            pltpu.VMEM((2, HALVES, 2, half, at), BF16),
            pltpu.VMEM((2, HALVES, 2, half, at), BF16),
            pltpu.VMEM((2, HALVES, half, at), BF16),
            pltpu.VMEM((2, HALVES, half, at), BF16),
            pltpu.VMEM((tab, width), BF16),
            pltpu.VMEM((tab, width), BF16),
            pltpu.VMEM((at, width), F32),
            pltpu.VMEM((at, width), F32),
            pltpu.VMEM((tab, width), F32),
            pltpu.VMEM((2, 2, ghost, width), BF16),
            pltpu.VMEM((2, ghost, width), BF16),
            pltpu.VMEM((at, width), BF16),
            pltpu.VMEM((at, width), BF16),
            pltpu.VMEM((at, width), F32),
            pltpu.VMEM((at, width), F32),
            pltpu.VMEM((at, width), F32),
            pltpu.VMEM((HALVES, half, at), F32),
            dma((2, 3)),
            dma((2, 2, HALVES, 3)),
            dma((2, 2, HALVES, zs - 1)),
            dma((2, 2, HALVES, zs - 1)),
            dma((2, 2, HALVES, 3)),
            dma((2, 2, 2)),
        ],
        compiler_params=pltpu.CompilerParams(
            collective_id=0, has_side_effects=True, vmem_limit_bytes=52 * 1024 * 1024
        ),
    )(
        features,
        positions,
        k_index,
        k_filter,
        w_in,
        w_out,
        w_msg,
        w_short,
        gamma.reshape(1, width),
        ghost_index,
        ghost_index.T,
        atom_count,
        src,
        src.T,
        edge_dist.reshape(at, NEIGH),
        cotangent,
    )


def solution(mesh):
    both = ("groups", "space")
    in_specs = (P(both, None), P(None, both)) + (P(),) * 7
    in_specs = in_specs + (P(both, None), P(both), P(both), P(both), P(both, None))
    out_specs = (P(both, None), P(both, None))
    return jax.shard_map(
        functools.partial(shards, mesh.shape["space"]),
        mesh=mesh,
        in_specs=in_specs,
        out_specs=out_specs,
        check_vma=False,
    )
```

```python
import functools
import math

import jax
import jax.numpy as jnp
from jax import lax
from jax.experimental import pallas as pl
from jax.experimental.pallas import tpu as pltpu
from jax.sharding import PartitionSpec as P

NEIGH = 16
QUAD = 4
HALVES = 2
ROWS = 16
WHOLE = 1.5 * 2.0**23
F32 = jnp.float32
BF16 = jnp.bfloat16

COS_FIT = (0.9999992251396179, -19.738981246948242, 64.92865753173828, -85.27162170410156, 58.79049301147461, -21.07110595703125)
SIN_FIT = (6.283185005187988, -41.341590881347656, 81.59994506835938, -76.61447143554688, 41.3428840637207, -12.471243858337402)


def horner(square, coefs):
    result = jnp.full_like(square, coefs[-1])
    for coef in coefs[-2::-1]:
        result = result * square + coef
    return result


def dot(left, right):
    return jnp.dot(left, right, preferred_element_type=F32)


def dot_trail(left, right):
    return lax.dot_general(left, right, (((1,), (1,)), ((), ())), preferred_element_type=F32)


def sigmoid(value):
    return 1.0 / (1.0 + jnp.exp(-value))


def silu_grad(value):
    sig = sigmoid(value)
    return sig * (1.0 + value * (1.0 - sig))


def one_hot(ids, axis, extent):
    shape = (ids.shape[0], extent) if axis == 1 else (extent, ids.shape[1])
    return jnp.where(lax.broadcasted_iota(jnp.int32, shape, axis) == ids, 1.0, 0.0).astype(BF16)


def kernel(
    n,
    scale,
    feat_ref,
    pos_ref,
    kidx_ref,
    kfilt_ref,
    win_ref,
    wout_ref,
    wmsg_ref,
    wshort_ref,
    gamma_ref,
    ghost_ref,
    count_ref,
    src_ref,
    dist_ref,
    cot_ref,
    mixed_ref,
    grad_ref,
    phase,
    kcol,
    pos_all,
    quad_all,
    z_send,
    z_recv,
    z_all,
    z_own,
    z_keep,
    sib_send,
    sib_recv,
    x_send,
    x_recv,
    table,
    hw,
    agg,
    grad_agg,
    grad_hw,
    ghost_send,
    ghost_back,
    masked_ref,
    glive_ref,
    wave_ref,
    long_ref,
    upstream_ref,
    mine,
    pos_sems,
    gather_sems,
    zr_sems,
    za_sems,
    quad_sems,
    ghost_sems,
):
    zs = n // QUAD
    at, width = feat_ref.shape
    kq = kidx_ref.shape[1] // QUAD
    kc = kq // zs
    ghost = ghost_ref.shape[1]
    half = width // HALVES
    me = lax.axis_index("space")
    q = lax.rem(me, QUAD)
    z = lax.div(me, QUAD)
    base = z * QUAD
    sib = q + 1 - 2 * lax.rem(q, 2)
    xp = lax.rem(q + 2, QUAD)
    diag = lax.rem(sib + 2, QUAD)
    right = lax.rem(me + 1, n)
    left = lax.rem(me + n - 1, n)

    def z_peer(step):
        return lax.rem(z + step, zs)

    barrier = pltpu.get_barrier_semaphore()
    peers = [base + sib, base + xp, left, right] + [z_peer(r) * QUAD + q for r in range(1, zs)]
    for peer in peers:
        pl.semaphore_signal(
            barrier, inc=1, device_id={"space": peer}, device_id_type=pl.DeviceIdType.MESH
        )

    def push(src, dst, sems, index, peer):
        return pltpu.make_async_remote_copy(
            src_ref=src,
            dst_ref=dst,
            send_sem=sems.at[(0,) + index],
            recv_sem=sems.at[(1,) + index],
            device_id={"space": peer},
            device_id_type=pl.DeviceIdType.MESH,
        )

    live = lax.broadcasted_iota(jnp.int32, (at, width), 0) < count_ref[0]
    live_f = jnp.where(live, 1.0, 0.0)
    masked = (feat_ref[...].astype(F32) * live_f).astype(BF16)
    masked_ref[...] = masked
    pos_all[q] = jnp.concatenate([pos_ref[...], jnp.zeros((5, at), F32)], axis=0)
    proj = dot(masked, win_ref[...]).astype(BF16)
    for h in range(HALVES):
        quad_all[0, h, q] = proj[:, h * half : (h + 1) * half]

    pl.semaphore_wait(barrier, len(peers))

    pos_copies = [
        push(pos_all.at[q], pos_all.at[q], pos_sems, (0,), base + sib),
        push(pos_all.at[q], pos_all.at[q], pos_sems, (1,), base + xp),
        push(pos_all.at[xp], pos_all.at[xp], pos_sems, (2,), base + sib),
    ]

    def gather_copies(rnd, h):
        buf = quad_all.at[rnd, h]
        return [
            push(buf.at[q], buf.at[q], gather_sems, (rnd, h, 0), base + sib),
            push(buf.at[q], buf.at[q], gather_sems, (rnd, h, 1), base + xp),
            push(buf.at[xp], buf.at[xp], gather_sems, (rnd, h, 2), base + sib),
        ]

    pos_copies[1].start()
    pos_copies[0].start()
    gathers = [gather_copies(0, h) for h in range(HALVES)]
    for copies in gathers:
        copies[1].start()
        copies[0].start()

    table[pl.ds(0, at), :] = masked
    ghost_pad = jnp.concatenate([ghost_ref[...].astype(F32), jnp.zeros((6, ghost), F32)], axis=0)
    ghost_col = ghost_pad.T.astype(jnp.int32)
    ghost_send[0, 0] = dot(one_hot(ghost_col[:, 0:1], 1, at), masked).astype(BF16)
    ghost_send[0, 1] = dot(one_hot(ghost_col[:, 1:2], 1, at), masked).astype(BF16)
    ghosts_out = [
        push(ghost_send.at[0, 0], table.at[pl.ds(at + ghost, ghost)], ghost_sems, (0, 0), left),
        push(ghost_send.at[0, 1], table.at[pl.ds(at, ghost)], ghost_sems, (0, 1), right),
    ]
    ghosts_out[0].start()
    ghosts_out[1].start()
    kq_rows = kidx_ref[:, pl.ds(pl.multiple_of(q * kq, 128), kq)].astype(F32)
    kcol[...] = jnp.concatenate([kq_rows, jnp.zeros((5, kq), F32)], axis=0).T
    glive_ref[...] = (cot_ref[...].astype(F32) * live_f).astype(BF16)
    pos_copies[1].wait()
    pos_copies[2].start()
    pos_copies[0].wait()
    upstream_ref[...] = dot_trail(glive_ref[...], wout_ref[...])
    grad_agg[...] = dot_trail(glive_ref[...], wshort_ref[...])
    pos_copies[2].wait()

    def fill_phase(j):
        def body(i, carry):
            first = pl.multiple_of(j * kc + i * ROWS, ROWS)
            ks = kcol[pl.ds(first, ROWS), :]
            row = pl.multiple_of(j * 2 * kc + i * ROWS, ROWS)
            k0 = jnp.broadcast_to(ks[:, 0:1], (ROWS, at))
            k1 = jnp.broadcast_to(ks[:, 1:2], (ROWS, at))
            k2 = jnp.broadcast_to(ks[:, 2:3], (ROWS, at))
            for slot in range(QUAD):
                columns = pl.ds(slot * at, at)
                turn = k0 * pos_all[slot, 0:1, :] + k1 * pos_all[slot, 1:2, :]
                turn = turn + k2 * pos_all[slot, 2:3, :]
                turn = turn - ((turn + WHOLE) - WHOLE)
                square = turn * turn
                phase[pl.ds(row, ROWS), columns] = horner(square, COS_FIT).astype(BF16)
                sines = (turn * horner(square, SIN_FIT)).astype(BF16)
                phase[pl.ds(pl.multiple_of(row + kc, ROWS), ROWS), columns] = sines
            return carry

        lax.fori_loop(0, kc // ROWS, body, 0)

    paired = zs == 4
    if paired:
        z1 = z + 1 - 2 * lax.rem(z, 2)
        z2 = lax.rem(z + 2, zs)
        targets = [lax.rem(z1 + 2, zs), z2, z1, z]
    else:
        targets = [z_peer(r) for r in range(1, zs)] + [z]

    def z_part(rnd, h, step):
        j = targets[step]
        rows = quad_all[rnd, h].reshape(QUAD * at, half)
        part = dot(phase[pl.ds(pl.multiple_of(j * 2 * kc, ROWS), 2 * kc), :], rows)
        if step == zs - 1:
            z_own[h] = part
            return []
        if paired and step == 1:
            z_keep[h] = part
            return []
        z_send[rnd, h, j] = part.astype(BF16)
        to, slot, index = (z1, step // 2, step // 2) if paired else (j, z, step)
        copy = push(
            z_send.at[rnd, h, j], z_recv.at[rnd, h, slot], zr_sems, (rnd, h, index), to * QUAD + q
        )
        copy.start()
        return [copy]

    def z_fold(rnd, h, copies):
        if not paired:
            return
        copies[0].wait()
        z_send[rnd, h, z2] = (z_keep[h] + z_recv[rnd, h, 0].astype(F32)).astype(BF16)
        copy = push(
            z_send.at[rnd, h, z2], z_recv.at[rnd, h, 2], zr_sems, (rnd, h, 2), z2 * QUAD + q
        )
        copy.start()
        copies.append(copy)

    def z_middle(rnd, h, copies):
        total = z_own[h]
        for r in range(1, zs):
            if paired and r == 1:
                continue
            copies[r - 1].wait()
            slot = r - 1 if paired else lax.rem(z + zs - r, zs)
            total = total + z_recv[rnd, h, slot].astype(F32)
        first = pl.multiple_of(q * kq + z * kc, ROWS)
        filt = kfilt_ref[pl.ds(first, kc), h * half : (h + 1) * half].astype(F32)
        z_all[rnd, h, z] = (jnp.concatenate([filt, filt], axis=0) * total * scale).astype(BF16)
        own = z_all.at[rnd, h, z]
        peers_of = [z1, z2] if paired else targets[:-1]
        out = []
        for index, peer in enumerate(peers_of):
            out.append(push(own, own, za_sems, (rnd, h, index), peer * QUAD + q))
            out[index].start()
        return out

    def z_relay(rnd, h, copies):
        if not paired:
            return
        copies[1].wait()
        slot = z_all.at[rnd, h, z2]
        copies.append(push(slot, slot, za_sems, (rnd, h, 2), z1 * QUAD + q))
        copies[2].start()

    def z_end(rnd, h, copies):
        for index, copy in enumerate(copies):
            if not (paired and index == 1):
                copy.wait()
        spectrum = z_all[rnd, h].reshape(2 * kq, half).T

        def section(slot):
            return dot(spectrum, phase[:, pl.ds(pl.multiple_of(slot * at, 128), at)])

        def sib_copy(k):
            return push(
                sib_send.at[rnd, h, k], sib_recv.at[rnd, h, k], quad_sems, (rnd, h, k), base + sib
            )

        across, beside = sib_copy(1), sib_copy(0)
        over = push(x_send.at[rnd, h], x_recv.at[rnd, h], quad_sems, (rnd, h, 2), base + xp)
        sib_send[rnd, h, 1] = section(diag).astype(BF16)
        across.start()
        part = section(xp)
        sib_send[rnd, h, 0] = section(sib).astype(BF16)
        beside.start()
        across.wait()
        x_send[rnd, h] = (part + sib_recv[rnd, h, 1].astype(F32)).astype(BF16)
        over.start()
        mine[h] = section(q)
        return beside, over

    def quad_sum(rnd, h, copies):
        copies[0].wait()
        copies[1].wait()
        total = mine[h] + sib_recv[rnd, h, 0].astype(F32)
        return (total + x_recv[rnd, h].astype(F32)).T

    def columns_of(h):
        return pl.ds(h * half, half)

    def back_start(h):
        wave = quad_sum(0, h, sums[h])
        wave_ref[:, columns_of(h)] = wave
        grad_wave = upstream_ref[:, columns_of(h)] * silu_grad(wave)
        quad_all[1, h, q] = grad_wave.astype(BF16)
        copies = gather_copies(1, h)
        copies[1].start()
        copies[0].start()
        return copies

    def forward_on(copies):
        copies[1].wait()
        copies[2].start()

    reduces = [[], []]
    for step in range(zs):
        fill_phase(targets[step])
        if step == 0:
            for copies in gathers:
                forward_on(copies)
            for copies in gathers:
                copies[0].wait()
                copies[2].wait()
        for h in range(HALVES):
            reduces[h] += z_part(0, h, step)
        if step == zs - 2:
            for h in range(HALVES):
                z_fold(0, h, reduces[h])

    spreads = [z_middle(0, h, reduces[h]) for h in range(HALVES)]

    dist = dist_ref[...]
    dist_sq = dist * dist
    turn = dist * 0.1
    live_col = jnp.where(
        lax.broadcasted_iota(jnp.int32, (at, NEIGH), 0) < count_ref[0], 1.0, 0.0
    )
    smooth = live_col * (0.5 * (horner(turn * turn, COS_FIT) + 1.0))
    gamma_neg = -gamma_ref[...]

    def radial(j):
        return smooth[:, j : j + 1] * jnp.exp(gamma_neg * dist_sq[:, j : j + 1])

    ghosts_out[0].wait()
    ghosts_out[1].wait()
    hw[...] = dot(table[...], wmsg_ref[...]).astype(BF16)
    for j in range(NEIGH):
        message = dot(one_hot(src_ref[:, j : j + 1], 1, at + 2 * ghost), hw[...]) * radial(j)
        agg[...] = message if j == 0 else agg[...] + message
        if j == 7:
            z_relay(0, 0, spreads[0])
    z_relay(0, 1, spreads[1])

    src_pad = jnp.concatenate([src_ref[...].astype(F32), jnp.zeros((at, 128 - NEIGH), F32)], axis=1)
    src_row = src_pad.T[:NEIGH].astype(jnp.int32)

    def short_back(first, last):
        for j in range(first, last):
            term = (grad_agg[...] * radial(j)).astype(BF16)
            part = dot(one_hot(src_row[j : j + 1, :], 0, at + 2 * ghost), term)
            grad_hw[...] = part if j == 0 else grad_hw[...] + part

    sums = [z_end(0, 0, spreads[0])]
    grad_agg[...] = grad_agg[...] * silu_grad(agg[...])
    short_back(0, 4)
    sums.append(z_end(0, 1, spreads[1]))
    gathers = [back_start(0)]
    short_back(4, 6)
    gathers.append(back_start(1))
    reduces = []
    forward_on(gathers[0])
    gathers[0][0].wait()
    gathers[0][2].wait()
    reduces.append(sum([z_part(1, 0, step) for step in range(zs)], []))
    forward_on(gathers[1])
    gathers[1][0].wait()
    gathers[1][2].wait()
    reduces.append(sum([z_part(1, 1, step) for step in range(zs)], []))
    for h in range(HALVES):
        z_fold(1, h, reduces[h])

    short_back(6, NEIGH)
    grad_table = dot_trail(grad_hw[...].astype(BF16), wmsg_ref[...])
    ghost_send[1, 0] = grad_table[at : at + ghost].astype(BF16)
    ghost_send[1, 1] = grad_table[at + ghost :].astype(BF16)
    ghosts_back = [
        push(ghost_send.at[1, 0], ghost_back.at[1], ghost_sems, (1, 0), left),
        push(ghost_send.at[1, 1], ghost_back.at[0], ghost_sems, (1, 1), right),
    ]
    ghosts_back[0].start()
    ghosts_back[1].start()
    long_ref[...] = grad_table[:at]
    spreads = [z_middle(1, h, reduces[h]) for h in range(HALVES)]

    wave = wave_ref[...]
    act = (wave * sigmoid(wave)).astype(BF16)
    short_act = (agg[...] * sigmoid(agg[...])).astype(BF16)
    z_relay(1, 0, spreads[0])
    mixed = masked_ref[...].astype(F32) + dot(short_act, wshort_ref[...])
    mixed = mixed + dot(act, wout_ref[...])
    mixed_ref[...] = (live_f * mixed).astype(BF16)
    ghosts_back[0].wait()
    ghosts_back[1].wait()
    own = long_ref[...]
    own = own + dot(one_hot(ghost_ref[0:1, :], 0, at), ghost_back[0])
    own = own + dot(one_hot(ghost_ref[1:2, :], 0, at), ghost_back[1])
    long_ref[...] = own + glive_ref[...].astype(F32)

    z_relay(1, 1, spreads[1])
    sums = [z_end(1, h, spreads[h]) for h in range(HALVES)]
    grad_proj = [quad_sum(1, h, sums[h]).astype(BF16) for h in range(HALVES)]
    total = long_ref[...] + dot_trail(jnp.concatenate(grad_proj, axis=1), win_ref[...])
    grad_ref[...] = (live_f * total).astype(BF16)


def shards(n, features, positions, k_index, k_filter, w_in, w_out, w_msg, w_short, gamma,
           ghost_index, atom_count, edge_src, edge_dist, cotangent):
    at, width = features.shape
    ghost = ghost_index.shape[1]
    kv = k_index.shape[1]
    zs = n // QUAD
    kq = kv // QUAD
    kc = kq // zs
    tab = at + 2 * ghost
    half = width // HALVES
    src = edge_src.reshape(at, NEIGH)
    vmem = pl.BlockSpec(memory_space=pltpu.VMEM)
    smem = pl.BlockSpec(memory_space=pltpu.SMEM)
    dma = pltpu.SemaphoreType.DMA
    return pl.pallas_call(
        functools.partial(kernel, n, 1.0 / math.sqrt(at * n)),
        out_shape=(
            jax.ShapeDtypeStruct((at, width), BF16),
            jax.ShapeDtypeStruct((at, width), BF16),
        ),
        in_specs=[vmem] * 10 + [smem] + [vmem] * 3,
        out_specs=(vmem, vmem),
        scratch_shapes=[
            pltpu.VMEM((2 * kq, QUAD * at), BF16),
            pltpu.VMEM((kq, 8), F32),
            pltpu.VMEM((QUAD, 8, at), F32),
            pltpu.VMEM((2, HALVES, QUAD, at, half), BF16),
            pltpu.VMEM((2, HALVES, zs, 2 * kc, half), BF16),
            pltpu.VMEM((2, HALVES, zs, 2 * kc, half), BF16),
            pltpu.VMEM((2, HALVES, zs, 2 * kc, half), BF16),
            pltpu.VMEM((HALVES, 2 * kc, half), F32),
            pltpu.VMEM((HALVES, 2 * kc, half), F32),
            pltpu.VMEM((2, HALVES, 2, half, at), BF16),
            pltpu.VMEM((2, HALVES, 2, half, at), BF16),
            pltpu.VMEM((2, HALVES, half, at), BF16),
            pltpu.VMEM((2, HALVES, half, at), BF16),
            pltpu.VMEM((tab, width), BF16),
            pltpu.VMEM((tab, width), BF16),
            pltpu.VMEM((at, width), F32),
            pltpu.VMEM((at, width), F32),
            pltpu.VMEM((tab, width), F32),
            pltpu.VMEM((2, 2, ghost, width), BF16),
            pltpu.VMEM((2, ghost, width), BF16),
            pltpu.VMEM((at, width), BF16),
            pltpu.VMEM((at, width), BF16),
            pltpu.VMEM((at, width), F32),
            pltpu.VMEM((at, width), F32),
            pltpu.VMEM((at, width), F32),
            pltpu.VMEM((HALVES, half, at), F32),
            dma((2, 3)),
            dma((2, 2, HALVES, 3)),
            dma((2, 2, HALVES, zs - 1)),
            dma((2, 2, HALVES, zs - 1)),
            dma((2, 2, HALVES, 3)),
            dma((2, 2, 2)),
        ],
        compiler_params=pltpu.CompilerParams(
            collective_id=0, has_side_effects=True, vmem_limit_bytes=52 * 1024 * 1024
        ),
    )(
        features,
        positions,
        k_index,
        k_filter,
        w_in,
        w_out,
        w_msg,
        w_short,
        gamma.reshape(1, width),
        ghost_index,
        atom_count,
        src,
        edge_dist.reshape(at, NEIGH),
        cotangent,
    )


def solution(mesh):
    both = ("groups", "space")
    in_specs = (P(both, None), P(None, both)) + (P(),) * 7
    in_specs = in_specs + (P(both, None), P(both), P(both), P(both), P(both, None))
    out_specs = (P(both, None), P(both, None))
    return jax.shard_map(
        functools.partial(shards, mesh.shape["space"]),
        mesh=mesh,
        in_specs=in_specs,
        out_specs=out_specs,
        check_vma=False,
    )
```
